1024 devices in a mesh: dp: 64 (over y_lo, z), expert: 16 (over y_hi, x, core).
Axes of the slice: x: 4, y: 8 (y_hi: 2, y_lo: 4; y = y_hi * 4 + y_lo), z: 16, core: 2. Of those that a mesh axis runs over, the one named last changes fastest.
Arguments:
- d_out: bfloat16 [131072, 4096], P(('dp', 'expert')), may hold values from -6 to 6
- logits: float32 [131072, 16], P(('dp', 'expert')), may hold values from -6 to 6
- routes: int32 [131072, 2], P(('dp', 'expert')), may hold values from 0 to 15, as said below
- slots: int32 [131072, 2], P(('dp', 'expert')), may hold values from 0 to 15, as said below
- state_map: bfloat16 [4096, 16], replicated, may hold values from -0.09375 to 0.09375
- channels: bfloat16 [16384, 8192], P(('dp', 'expert')), may hold values from -0.5 to 0.5
Outputs:
- expert_grads: bfloat16 [64, 16, 16, 16, 4096], P('dp', 'expert')
- mamba_grad: float32 [16, 8192], P(None, 'expert')
The draws below stay inside these ranges and needn't reach their ends.
Inputs may be any that keep to these rules, and one draw needn't show every extreme that they name: `routes`: on one device a token's two experts differ, every expert is named by exactly 16 of the device's choices, and a token's second expert is a fixed function of its first on each device. On one device the choices of one expert hold the slots 0 to 15, each once.
All inputs are finite; a program needn't handle non-finite values.
Results may differ from the reference program's by a relative error of at most 0.0032.
Values may be sent and summed in bfloat16 or wider, within the bound.
A program may use at most 32 MiB of HBM per device.

```python
import jax
import jax.numpy as jnp
from jax import lax

D = 4096
INNER = 8192
NSTATE = 16
TOK_DEV = 128
EXPERTS = 16
CAP = 16
TOKENS = 131072
MAMBA_DEV = 16
MAMBA_TOKENS = 16384
N_DP = 64
N_EXPERT = 16


def route_table(key):
    device_count = TOKENS // TOK_DEV

    def per_device(device):
        device_key = jax.random.fold_in(key, device)
        key_first, key_cycle, key_order = jax.random.split(device_key, 3)
        first_pick = jax.random.permutation(key_first, jnp.arange(TOK_DEV, dtype=jnp.int32) % EXPERTS)
        cyclic = jax.random.permutation(key_cycle, EXPERTS).astype(jnp.int32)
        position = jnp.argsort(cyclic).astype(jnp.int32)
        successor = cyclic[(position + 1) % EXPERTS]
        second = successor[first_pick]
        chosen = jnp.stack([first_pick, second], axis=1)
        flat_pick = chosen.reshape(-1)
        ticket = jax.random.permutation(key_order, 2 * TOK_DEV).astype(jnp.int32)
        scores = flat_pick * (2 * TOK_DEV) + ticket
        ordering = jnp.argsort(scores).astype(jnp.int32)
        ranking = jnp.zeros((2 * TOK_DEV,), jnp.int32).at[ordering].set(jnp.arange(2 * TOK_DEV, dtype=jnp.int32))
        slot_index = ranking - flat_pick * CAP
        return (chosen, slot_index.reshape(TOK_DEV, 2))
    chosen, slot_index = jax.vmap(per_device)(jnp.arange(device_count, dtype=jnp.int32))
    return (chosen.reshape(TOKENS, 2), slot_index.reshape(TOKENS, 2))


def draw_routes(key, part):
    routed, placed = route_table(key)
    return routed


def draw_slots(key, part):
    routed, placed = route_table(key)
    return placed


def with_spikes(array, own_key, source, target, parts, factor):
    def block_of(dim):
        return (jnp.arange(array.shape[dim]) // (array.shape[dim] // parts)).reshape((-1,) + (1,) * (array.ndim - 1 - dim))

    first = jax.random.permutation(own_key, parts)[block_of(target)]
    other_side = (block_of(target) + parts // 2) % parts
    return jnp.where((block_of(source) == first) | (block_of(source) == other_side), factor * array, array)


def shard_levels(key, dims, cuts, low, largest):
    level, own = 1.0, jax.random.fold_in(key, 6)
    for axis_at, parts in cuts:
        heights = jnp.exp(jax.random.uniform(jax.random.fold_in(own, axis_at), (parts,), jnp.float32, low / len(cuts), largest / len(cuts)))
        level = level * jnp.repeat(heights, dims[axis_at] // parts).reshape([-1 if axis == axis_at else 1 for axis in range(len(dims))])
    return level


def normal_values(own_key, dims, deviation, bound, cuts=(), kind=jnp.bfloat16):
    drawn = jax.random.normal(own_key, dims, jnp.float32) * deviation
    if len(cuts) > 0:
        drawn = shard_levels(own_key, dims, cuts, -0.22, 0.18) * drawn
    return jnp.clip(drawn, min=-bound, max=bound).astype(kind)


def noise_with(own_key, dims, scale, bound, cuts, heavy, held_as=jnp.bfloat16):
    drawn = scale * jax.random.normal(own_key, dims, jnp.float32)
    if cuts:
        drawn = drawn * shard_levels(own_key, dims, cuts, -0.22, 0.18)
    return jnp.clip(with_spikes(drawn, jax.random.fold_in(own_key, 3), *heavy), -bound, bound).astype(held_as)


def setup_inputs(seed: int = 0) -> dict:
    arg_keys = jax.random.split(jax.random.key(seed), 7)
    return {
        "d_out": normal_values(arg_keys[0], (TOKENS, D), 1.0, 6.0, ((0, 1024),)),
        "logits": normal_values(arg_keys[1], (TOKENS, EXPERTS), 1.5, 6.0, ((0, 1024),), jnp.float32),
        "routes": draw_routes(jax.random.fold_in(arg_keys[6], 71), 0),
        "slots": draw_slots(jax.random.fold_in(arg_keys[6], 71), 0),
        "state_map": normal_values(arg_keys[4], (D, NSTATE), D ** -0.5, 0.09375),
        "channels": noise_with(arg_keys[5], (MAMBA_TOKENS, INNER), (1.0 / MAMBA_TOKENS ** 0.5), 0.5, ((0, 1024),), (0, 1, 1024, 6.0)),
    }


def pack_device(cotangent, logit_rows, route_rows, slot_rows):
    expert_ids = jnp.arange(EXPERTS, dtype=jnp.int32)
    selected = jnp.sum(jnp.where(route_rows[:, :, None] == expert_ids[None, None, :], logit_rows[:, None, :], jnp.float32(0.0)), axis=2)
    weights = jnp.stack([jax.nn.sigmoid(selected[:, 0] - selected[:, 1]), jax.nn.sigmoid(selected[:, 1] - selected[:, 0])], axis=1)
    pieces = (weights[:, :, None] * cotangent[:, None, :].astype(jnp.float32)).astype(jnp.bfloat16)
    target = route_rows * CAP + slot_rows
    one_hot = (target[None, :, :] == jnp.arange(EXPERTS * CAP, dtype=jnp.int32)[:, None, None]).astype(jnp.float32)
    buffer = jnp.einsum("rtk,tkd->rd", one_hot, pieces.astype(jnp.float32))
    return buffer.astype(jnp.bfloat16).reshape(EXPERTS, CAP, D)


def reference(d_out, logits, routes, slots, state_map, channels):
    grouped = d_out.reshape(N_DP, N_EXPERT, TOK_DEV, D)
    logit_groups = logits.reshape(N_DP, N_EXPERT, TOK_DEV, EXPERTS)
    route_groups = routes.reshape(N_DP, N_EXPERT, TOK_DEV, 2)
    slot_groups = slots.reshape(N_DP, N_EXPERT, TOK_DEV, 2)

    def per_group(inputs):
        return jax.vmap(pack_device)(*inputs)

    packed = lax.map(per_group, (grouped, logit_groups, route_groups, slot_groups))
    expert_grads = jnp.transpose(packed, (0, 2, 1, 3, 4))

    cot_groups = grouped[:, :, :MAMBA_DEV, :].reshape(N_DP, N_EXPERT * MAMBA_DEV, D)
    channel_groups = channels.reshape(N_DP, N_EXPERT * MAMBA_DEV, INNER)

    def accumulate(total, inputs):
        cot_rows, channel_rows = inputs
        state_cot = jnp.dot(cot_rows, state_map, preferred_element_type=jnp.float32).astype(jnp.bfloat16)
        term = jnp.dot(state_cot.T, channel_rows, preferred_element_type=jnp.float32)
        return total + term, None

    mamba_grad, unused = lax.scan(accumulate, jnp.zeros((NSTATE, INNER), jnp.float32), (cot_groups, channel_groups))
    return expert_grads, mamba_grad
```

```python
import jax
import jax.numpy as jnp
from jax import lax
from jax.experimental import pallas as pl
from jax.experimental.pallas import tpu as pltpu
from jax.sharding import PartitionSpec as P

MESH = pl.DeviceIdType.MESH
NX, NY, NZ, NC = 4, 8, 16, 2
EXPERTS, CAP, D = 16, 16, 4096
ROW = NX * NC
BLOCK = 512
TILE = 512

FAR = [(1, dx, dc) for dx in (2, 1, 3, 0) for dc in (0, 1)]
NEAR = [(0, dx, dc) for dx in (2, 1, 3, 0) for dc in (0, 1) if (dx, dc) != (0, 0)]
BULK = [pair[i] for i in range(8) for pair in (FAR, NEAR) if i < len(pair)]
CUTS = (4, 8, 11)
ALONG_Z = [s * k % NZ for k in range(1, 9) for s in (1, -1) if not (k == 8 and s < 0)]
ALONG_Y = (4, 3, 5, 2, 6, 1, 7)


def kernel(
    d_hbm, logits_hbm, routes_hbm, slots_hbm, map_hbm, channels_hbm,
    out, grad,
    d, logits, routes, slots, state_map, channels, pack,
    rows_out, rows_in, z_out, z_in, y_out, y_in, f_out, f_in,
    load_sem, own_sem, b_send, b_recv, r_send, r_recv, z_send, z_recv, y_send, y_recv, f_send, f_recv,
):
    dp, me = lax.axis_index("dp"), lax.axis_index("expert")
    z, y_lo = lax.rem(dp, NZ), dp // NZ
    y_hi, row = me // ROW, lax.rem(me, ROW)
    x, c = row // NC, lax.rem(row, NC)
    y = y_hi * 4 + y_lo

    def peer(dy, dx, dc):
        return (
            lax.rem(y_hi + dy, 2) * ROW + lax.rem(x + dx, NX) * NC + lax.rem(c + dc, NC)
        )

    def at_z(other):
        return (y_lo * NZ + other, me)

    def at_y(other):
        return (lax.rem(other, 4) * NZ + z, (other // 4) * ROW + row)

    barrier = pltpu.get_barrier_semaphore()

    def greet(device):
        pl.semaphore_signal(barrier, inc=1, device_id=device, device_id_type=MESH)

    greeted = 0
    for offsets in BULK:
        greet((dp, peer(*offsets)))
        greeted += 1
    for k in ALONG_Z:
        greet(at_z(lax.rem(z + k, NZ)))
        greeted += 1
    for k in ALONG_Y:
        if k != 4:
            greet(at_y(lax.rem(y + k, NY)))
            greeted += 1

    loads = [
        pltpu.make_async_copy(source, target, load_sem.at[i])
        for i, (source, target) in enumerate(
            [
                (logits_hbm, logits),
                (routes_hbm, routes),
                (slots_hbm, slots),
                (d_hbm, d),
                (channels_hbm, channels),
                (map_hbm, state_map),
            ]
        )
    ]
    for load in loads:
        load.start()
    for load in loads[:3]:
        load.wait()

    expert_ids = lax.broadcasted_iota(jnp.int32, (EXPERTS, 128), 0)
    picked = [
        jnp.sum(
            jnp.where(expert_ids == routes[k : k + 1, :], logits[...], 0.0),
            axis=0,
            keepdims=True,
        )
        for k in range(2)
    ]
    weights = [
        jax.nn.sigmoid(picked[0] - picked[1]),
        jax.nn.sigmoid(picked[1] - picked[0]),
    ]
    target = [routes[k : k + 1, :] * CAP + slots[k : k + 1, :] for k in range(2)]

    def route(half):
        ids = lax.broadcasted_iota(jnp.int32, (128, 128), 0) + half * 128
        hit = [ids == target[k] for k in range(2)]
        chosen = jnp.where(hit[0] | hit[1], 1.0, 0.0).astype(jnp.bfloat16)
        scale = jnp.where(hit[0], weights[0], 0.0) + jnp.where(hit[1], weights[1], 0.0)
        return chosen, jnp.sum(scale, axis=1, keepdims=True)

    def pack_half(half):
        chosen, scale = route(half)
        for i in range(D // TILE):
            columns = slice(i * TILE, (i + 1) * TILE)
            rows = jnp.dot(chosen, d[:, columns], preferred_element_type=jnp.float32)
            pack[pl.ds(half * 8, 8), :, columns] = (
                (rows * scale).astype(jnp.bfloat16).reshape(8, CAP, TILE)
            )

    loads[3].wait()
    pack_half(1 - y_hi)

    loads[4].wait()
    loads[5].wait()
    state_cot = lax.dot_general(
        d[0:16, :], state_map[...], (((1,), (1,)), ((), ())),
        preferred_element_type=jnp.float32,
    ).astype(jnp.bfloat16)
    spread = (
        lax.broadcasted_iota(jnp.int32, (16, 128), 0)
        == lax.broadcasted_iota(jnp.int32, (16, 128), 1)
    ).astype(jnp.bfloat16)
    wide = jnp.dot(state_cot, spread, preferred_element_type=jnp.float32).astype(
        jnp.bfloat16
    )
    for i in range(ROW):
        for b in range(2):
            begin = (b * ROW + i) * BLOCK
            rows_out[i, :, b * BLOCK : (b + 1) * BLOCK] = channels[:, begin : begin + BLOCK]
        rows_out[i, :, 2 * BLOCK :] = wide

    pl.semaphore_wait(barrier, greeted)

    def send(source, destination, send_sem, recv_sem, device):
        copy = pltpu.make_async_remote_copy(
            src_ref=source,
            dst_ref=destination,
            send_sem=send_sem,
            recv_sem=recv_sem,
            device_id=device,
            device_id_type=MESH,
        )
        return copy

    def bulk(offsets):
        other = peer(*offsets)
        return send(pack.at[other], out.at[me], b_send.at[other], b_recv.at[me], (dp, other))

    def bulk_in(offsets):
        other = peer(*offsets)
        return send(pack.at[other], out.at[other], b_send.at[other], b_recv.at[other], (dp, other))

    for offsets in FAR[:1]:
        bulk(offsets).start()
    for _, dx, dc in NEAR:
        other = lax.rem(x + dx, NX) * NC + lax.rem(c + dc, NC)
        send(
            rows_out.at[other], rows_in.at[row], r_send.at[other], r_recv.at[row],
            (dp, y_hi * ROW + other),
        ).start()
    rows_in[row] = rows_out[row]
    pack_half(y_hi)
    own = pltpu.make_async_copy(pack.at[me], out.at[me], own_sem)
    own.start()
    for offsets in BULK[1 : CUTS[0]]:
        bulk(offsets).start()

    for _, dx, dc in NEAR:
        other = lax.rem(x + dx, NX) * NC + lax.rem(c + dc, NC)
        copy = send(
            rows_out.at[other], rows_in.at[other], r_send.at[other], r_recv.at[other],
            (dp, y_hi * ROW + other),
        )
        copy.wait_recv()
    cot = rows_in[:, :, 2 * BLOCK :].reshape(ROW * 16, 128)
    cot = cot.astype(jnp.float32).T[0:16, :].astype(jnp.bfloat16)
    partial = jnp.dot(
        cot, rows_in[:, :, : 2 * BLOCK].reshape(ROW * 16, 2 * BLOCK),
        preferred_element_type=jnp.float32,
    )
    for h in range(2):
        for q in range(8):
            z_out[h * 8 + q] = partial[h * 8 : (h + 1) * 8, q * 128 : (q + 1) * 128]
    for k in ALONG_Z:
        other = lax.rem(z + k, NZ)
        send(z_out.at[other], z_in.at[z], z_send.at[other], z_recv.at[z], at_z(other)).start()
    for offsets in BULK[CUTS[0] : CUTS[1]]:
        bulk(offsets).start()
    z_in[z] = z_out[z]

    for k in ALONG_Z:
        other = lax.rem(z + k, NZ)
        send(z_out.at[other], z_in.at[other], z_send.at[other], z_recv.at[other], at_z(other)).wait_recv()
    total = jnp.sum(z_in[...], axis=0)
    y_out[...] = total
    half = lax.rem(z, 8) // 4
    for k in ALONG_Y:
        other = lax.rem(y + k, NY)

        @pl.when(other // 4 == half)
        def _():
            send(y_out, y_in.at[y], y_send.at[other], y_recv.at[y], at_y(other)).start()

    for offsets in BULK[CUTS[1] : CUTS[2]]:
        bulk(offsets).start()
    y_in[y] = total

    @pl.when(y_hi == half)
    def _():
        for k in ALONG_Y:
            other = lax.rem(y + k, NY)
            send(y_out, y_in.at[other], y_send.at[other], y_recv.at[other], at_y(other)).wait_recv()
        summed = jnp.sum(y_in[...], axis=0)
        f_out[...] = summed
        for k in ALONG_Z:
            other = lax.rem(z + k, NZ)
            send(f_out, f_in.at[z], f_send.at[other], f_recv.at[z], at_z(other)).start()
        f_in[z] = summed

    for offsets in BULK[CUTS[2] :]:
        bulk(offsets).start()

    for h in range(2):
        for q in range(4):
            other = h * 8 + y_hi * 4 + q

            @pl.when(other != z)
            def _():
                send(f_out, f_in.at[other], f_send.at[other], f_recv.at[other], at_z(other)).wait_recv()

    for h in range(2):
        for q in range(4):
            grad[h * 8 : (h + 1) * 8, q * 128 : (q + 1) * 128] = f_in[h * 8 + y_hi * 4 + q]

    for _, dx, dc in NEAR:
        other = lax.rem(x + dx, NX) * NC + lax.rem(c + dc, NC)
        send(
            rows_out.at[other], rows_in.at[row], r_send.at[other], r_recv.at[row],
            (dp, y_hi * ROW + other),
        ).wait_send()
    for k in ALONG_Z:
        other = lax.rem(z + k, NZ)
        send(z_out.at[other], z_in.at[z], z_send.at[other], z_recv.at[z], at_z(other)).wait_send()
    for k in ALONG_Y:
        other = lax.rem(y + k, NY)

        @pl.when(other // 4 == half)
        def _():
            send(y_out, y_in.at[y], y_send.at[other], y_recv.at[y], at_y(other)).wait_send()

    @pl.when(y_hi == half)
    def _():
        for k in ALONG_Z:
            other = lax.rem(z + k, NZ)
            send(f_out, f_in.at[z], f_send.at[other], f_recv.at[z], at_z(other)).wait_send()

    own.wait()
    for offsets in BULK:
        bulk(offsets).wait_send()
        bulk_in(offsets).wait_recv()


def shards(d_out, logits, routes, slots, state_map, channels):
    anywhere = pl.BlockSpec(memory_space=pl.ANY)
    in_hbm = pl.BlockSpec(memory_space=pltpu.HBM)
    bf16, f32 = jnp.bfloat16, jnp.float32
    dma = pltpu.SemaphoreType.DMA
    received, grad = pl.pallas_call(
        kernel,
        out_shape=(
            jax.ShapeDtypeStruct((EXPERTS, CAP, D), bf16),
            jax.ShapeDtypeStruct((16, BLOCK), f32),
        ),
        in_specs=[in_hbm] * 6,
        out_specs=(anywhere, pl.BlockSpec(memory_space=pltpu.VMEM)),
        scratch_shapes=[
            pltpu.VMEM((128, D), bf16),
            pltpu.VMEM((EXPERTS, 128), f32),
            pltpu.VMEM((2, 128), jnp.int32),
            pltpu.VMEM((2, 128), jnp.int32),
            pltpu.VMEM((16, D), bf16),
            pltpu.VMEM((16, EXPERTS * BLOCK), bf16),
            pltpu.VMEM((EXPERTS, CAP, D), bf16),
            pltpu.VMEM((ROW, 16, 2 * BLOCK + 128), bf16),
            pltpu.VMEM((ROW, 16, 2 * BLOCK + 128), bf16),
            pltpu.VMEM((NZ, 8, 128), f32),
            pltpu.VMEM((NZ, 8, 128), f32),
            pltpu.VMEM((8, 128), f32),
            pltpu.VMEM((NY, 8, 128), f32),
            pltpu.VMEM((8, 128), f32),
            pltpu.VMEM((NZ, 8, 128), f32),
            dma((6,)), dma,
            dma((EXPERTS,)), dma((EXPERTS,)),
            dma((ROW,)), dma((ROW,)),
            dma((NZ,)), dma((NZ,)),
            dma((NY,)), dma((NY,)),
            dma((NZ,)), dma((NZ,)),
        ],
        compiler_params=pltpu.CompilerParams(
            collective_id=0, has_side_effects=True, vmem_limit_bytes=24 << 20
        ),
        cost_estimate=pl.CostEstimate(
            flops=300_000_000, bytes_accessed=8_000_000, transcendentals=256
        ),
    )(d_out, logits.T, routes.T, slots.T, state_map.T, channels)
    return received[None, None], grad


def solution(mesh):
    return jax.shard_map(
        shards,
        mesh=mesh,
        in_specs=(
            P(("dp", "expert"), None),
            P(("dp", "expert"), None),
            P(("dp", "expert"), None),
            P(("dp", "expert"), None),
            P(),
            P(("dp", "expert"), None),
        ),
        out_specs=(P("dp", "expert", None, None, None), P(None, "expert")),
        check_vma=False,
    )
```

```python
import jax
import jax.numpy as jnp
from jax import lax
from jax.experimental import pallas as pl
from jax.experimental.pallas import tpu as pltpu
from jax.sharding import PartitionSpec as P

MESH = pl.DeviceIdType.MESH
NX, NY, NZ, NC = 4, 8, 16, 2
EXPERTS, CAP, D = 16, 16, 4096
ROW = NX * NC
BLOCK = 512
TILE = 512

FAR = [(1, dx, dc) for dx in (2, 1, 3, 0) for dc in (0, 1)]
NEAR = [(0, dx, dc) for dx in (2, 1, 3, 0) for dc in (0, 1) if (dx, dc) != (0, 0)]
PEERS = FAR + NEAR
PARTS = 2
MIX = [pair[i] for i in range(8) for pair in (FAR, NEAR) if i < len(pair)]
BULK = [(*offsets, q) for q in range(PARTS) for offsets in MIX]
FIRST = 1
EXTRA = ((14, 14, 4),)
CUTS = (14, 26, 30)
DO_M = True
ALONG_Z = [s * k % NZ for k in range(1, 9) for s in (1, -1) if not (k == 8 and s < 0)]
ROLES = 4
ALONG_Y = (4, 3, 5, 2, 6, 1, 7)


def kernel(
    d_hbm, logits_hbm, routes_hbm, slots_hbm, map_hbm, channels_hbm,
    out, grad,
    d, logits, routes, slots, state_map, channels, pack,
    rows_out, rows_in, z_out, z_in, y_out, y_in, f_out, f_in,
    load_sem, own_sem, later, first, line, b_send, b_recv, r_send, r_recv, z_send, z_recv, y_send, y_recv, f_send, f_recv,
):
    dp, me = lax.axis_index("dp"), lax.axis_index("expert")
    z, y_lo = lax.rem(dp, NZ), dp // NZ
    y_hi, row = me // ROW, lax.rem(me, ROW)
    x, c = row // NC, lax.rem(row, NC)
    y = y_hi * 4 + y_lo

    def peer(dy, dx, dc, part=0):
        return (
            lax.rem(y_hi + dy, 2) * ROW + lax.rem(x + dx, NX) * NC + lax.rem(c + dc, NC)
        )

    def at_z(other):
        return (y_lo * NZ + other, me)

    def at_y(other):
        return (lax.rem(other, 4) * NZ + z, (other // 4) * ROW + row)

    barrier = pltpu.get_barrier_semaphore()

    def greet(device):
        pl.semaphore_signal(barrier, inc=1, device_id=device, device_id_type=MESH)

    corner = (row == 0) & (y == 0)
    rank = jnp.where(corner, lax.rem(z + NZ - 1, NZ), z)

    for offsets in PEERS:

        @pl.when(me != 0)
        def _():
            greet((dp, peer(*offsets)))

    for k in ALONG_Y:
        if k != 4:

            @pl.when(y != 0)
            def _():
                greet(at_y(lax.rem(y + k, NY)))

    for k in range(1, NZ):

        @pl.when(rank + k < NZ)
        def _():
            greet(at_z(lax.rem(z + k, NZ)))

    greeted = rank + jnp.where(me == 0, 15, 14) + jnp.where((y == 0) | (y == 4), 6, 5)

    loads = [
        pltpu.make_async_copy(source, target, load_sem.at[i])
        for i, (source, target) in enumerate(
            [
                (logits_hbm, logits),
                (routes_hbm, routes),
                (slots_hbm, slots),
                (d_hbm, d),
                (channels_hbm, channels),
                (map_hbm, state_map),
            ]
        )
    ]
    for load in loads:
        load.start()
    for load in loads[:3]:
        load.wait()

    expert_ids = lax.broadcasted_iota(jnp.int32, (EXPERTS, 128), 0)
    picked = [
        jnp.sum(
            jnp.where(expert_ids == routes[k : k + 1, :], logits[...], 0.0),
            axis=0,
            keepdims=True,
        )
        for k in range(2)
    ]
    weights = [
        jax.nn.sigmoid(picked[0] - picked[1]),
        jax.nn.sigmoid(picked[1] - picked[0]),
    ]
    target = [routes[k : k + 1, :] * CAP + slots[k : k + 1, :] for k in range(2)]

    def route(half):
        ids = lax.broadcasted_iota(jnp.int32, (128, 128), 0) + half * 128
        hit = [ids == target[k] for k in range(2)]
        chosen = jnp.where(hit[0] | hit[1], 1.0, 0.0).astype(jnp.bfloat16)
        scale = jnp.where(hit[0], weights[0], 0.0) + jnp.where(hit[1], weights[1], 0.0)
        return chosen, jnp.sum(scale, axis=1, keepdims=True)

    def pack_half(half):
        chosen, scale = route(half)
        for i in range(D // TILE):
            columns = slice(i * TILE, (i + 1) * TILE)
            rows = jnp.dot(chosen, d[:, columns], preferred_element_type=jnp.float32)
            pack[pl.ds(half * 8, 8), :, columns] = (
                (rows * scale).astype(jnp.bfloat16).reshape(8, CAP, TILE)
            )

    loads[3].wait()
    pack_half(1 - y_hi)

    loads[4].wait()
    loads[5].wait()
    state_cot = lax.dot_general(
        d[0:16, :], state_map[...], (((1,), (1,)), ((), ())),
        preferred_element_type=jnp.float32,
    ).astype(jnp.bfloat16)
    spread = (
        lax.broadcasted_iota(jnp.int32, (16, 128), 0)
        == lax.broadcasted_iota(jnp.int32, (16, 128), 1)
    ).astype(jnp.bfloat16)
    wide = jnp.dot(state_cot, spread, preferred_element_type=jnp.float32).astype(
        jnp.bfloat16
    )
    for i in range(ROW):
        for b in range(2):
            begin = (b * ROW + i) * BLOCK
            rows_out[i, :, b * BLOCK : (b + 1) * BLOCK] = channels[:, begin : begin + BLOCK]
        rows_out[i, :, 2 * BLOCK :] = wide

    pl.semaphore_wait(barrier, greeted)

    def tell(semaphore, device):
        pl.semaphore_signal(semaphore, inc=1, device_id=device, device_id_type=MESH)

    for offsets in PEERS:

        @pl.when(me == 0)
        def _():
            tell(first, (dp, peer(*offsets)))

    for k in ALONG_Y:
        if k != 4:

            @pl.when(y == 0)
            def _():
                tell(line, at_y(lax.rem(y + k, NY)))

    for k in range(1, NZ):

        @pl.when(k <= rank)
        def _():
            tell(later, at_z(lax.rem(z + NZ - k, NZ)))

    def send(source, destination, send_sem, recv_sem, device):
        copy = pltpu.make_async_remote_copy(
            src_ref=source,
            dst_ref=destination,
            send_sem=send_sem,
            recv_sem=recv_sem,
            device_id=device,
            device_id_type=MESH,
        )
        return copy

    def block(offsets, at):
        return to(peer(*offsets), offsets[3], at)

    def to(other, q, at):
        columns = pl.ds(q * (D // PARTS), D // PARTS)
        return send(
            pack.at[other, :, columns], out.at[at(other), :, columns],
            b_send.at[other, q], b_recv.at[at(other), q], (dp, other),
        )

    def to_first(q):
        return to(0, q, lambda other: me)

    def bulk(offsets):
        return block(offsets, lambda other: me)

    def bulk_in(offsets):
        return block(offsets, lambda other: other)

    def start(parts):
        for offsets in parts:

            @pl.when(peer(*offsets) != 0)
            def _():
                bulk(offsets).start()

    start(BULK[:FIRST])
    def across(other):
        return send(
            rows_out.at[other], rows_in.at[row], r_send.at[other], r_recv.at[row],
            (dp, y_hi * ROW + other),
        )

    for _, dx, dc in NEAR:
        other = lax.rem(x + dx, NX) * NC + lax.rem(c + dc, NC)

        @pl.when(y_hi * ROW + other != 0)
        def _():
            across(other).start()

    rows_in[row] = rows_out[row]
    pack_half(y_hi)
    own = pltpu.make_async_copy(pack.at[me], out.at[me], own_sem)
    own.start()
    start(BULK[FIRST : CUTS[0]])

    def extra(i, early):
        begin, end, below = EXTRA[i]

        @pl.when((z < below) == early)
        def _():
            start(BULK[begin:end])

    for i in range(len(EXTRA)):
        extra(i, True)

    @pl.when(me != 0)
    def _():
        pl.semaphore_wait(first, 1)

        @pl.when(y_hi == 0)
        def _():
            across(0).start()

        for q in range(PARTS):
            to_first(q).start()


    for _, dx, dc in NEAR:
        other = lax.rem(x + dx, NX) * NC + lax.rem(c + dc, NC)
        copy = send(
            rows_out.at[other], rows_in.at[other], r_send.at[other], r_recv.at[other],
            (dp, y_hi * ROW + other),
        )
        copy.wait_recv()
    cot = rows_in[:, :, 2 * BLOCK :].reshape(ROW * 16, 128)
    cot = cot.astype(jnp.float32).T[0:16, :].astype(jnp.bfloat16)
    partial = jnp.dot(
        cot, rows_in[:, :, : 2 * BLOCK].reshape(ROW * 16, 2 * BLOCK),
        preferred_element_type=jnp.float32,
    )
    for p in range(16):
        h, q = p // 8, p % 8
        z_out[p // 4, p % 4] = partial[h * 8 : (h + 1) * 8, q * 128 : (q + 1) * 128]

    adds = z < ROLES
    wait_now = adds | corner

    @pl.when(wait_now & (rank < NZ - 1))
    def _():
        pl.semaphore_wait(later, NZ - 1 - rank)

    def along(to):
        return send(z_out.at[to], z_in.at[z], z_send.at[to], z_recv.at[z], at_z(to))

    for to_z in range(ROLES):

        @pl.when(z != to_z)
        def _():
            along(to_z).start()

    for i in range(len(EXTRA)):
        extra(i, False)
    start(BULK[EXTRA[-1][1] : CUTS[1]])
    @pl.when((y != 0) & (y != 4))
    def _():
        pl.semaphore_wait(line, 1)

    half = lax.rem(z, 2)

    def upright(other):
        return send(y_out, y_in.at[y], y_send.at[other], y_recv.at[y], at_y(other))

    @pl.when(adds)
    def _():
        z_in[z] = z_out[lax.rem(z, ROLES)]
        for k in ALONG_Z:
            other = lax.rem(z + k, NZ)
            send(z_out.at[0], z_in.at[other], z_send.at[0], z_recv.at[other], at_z(other)).wait_recv()
        total = jnp.sum(z_in[...], axis=0)
        y_out[...] = total
        for k in ALONG_Y:
            other = lax.rem(y + k, NY)

            @pl.when(other // 4 == half)
            def _():
                upright(other).start()

        y_in[y] = total

    start(BULK[CUTS[1] : CUTS[2]])

    gives = adds & (y_hi == half)

    def back(other):
        return send(f_out, f_in.at[z // 2], f_send.at[other], f_recv.at[z // 2], at_z(other))

    @pl.when(gives)
    def _():
        for k in ALONG_Y:
            other = lax.rem(y + k, NY)
            send(y_out, y_in.at[other], y_send.at[other], y_recv.at[other], at_y(other)).wait_recv()
        summed = jnp.sum(y_in[...], axis=0)
        f_out[...] = summed
        for k in ALONG_Z:
            back(lax.rem(z + k, NZ)).start()
        f_in[z // 2] = summed

    start(BULK[CUTS[2] :])

    for h in range(2):
        giver = 2 * h + y_hi

        @pl.when(giver != z)
        def _():
            send(f_out, f_in.at[h], f_send.at[0], f_recv.at[h], at_z(giver)).wait_recv()

    for p in range(8):
        h, q = p // 4, p % 4
        grad[h * 8 : (h + 1) * 8, q * 128 : (q + 1) * 128] = f_in[h, q]

    @pl.when(jnp.logical_not(wait_now) & (rank < NZ - 1))
    def _():
        pl.semaphore_wait(later, NZ - 1 - rank)

    for _, dx, dc in NEAR:
        across(lax.rem(x + dx, NX) * NC + lax.rem(c + dc, NC)).wait_send()
    for to_z in range(ROLES):

        @pl.when(z != to_z)
        def _():
            along(to_z).wait_send()

    for k in ALONG_Y:
        other = lax.rem(y + k, NY)

        @pl.when(adds & (other // 4 == half))
        def _():
            upright(other).wait_send()

    @pl.when(gives)
    def _():
        for k in ALONG_Z:
            back(lax.rem(z + k, NZ)).wait_send()

    own.wait()
    for offsets in BULK:
        bulk(offsets).wait_send()
        bulk_in(offsets).wait_recv()


def shards(d_out, logits, routes, slots, state_map, channels):
    anywhere = pl.BlockSpec(memory_space=pl.ANY)
    in_hbm = pl.BlockSpec(memory_space=pltpu.HBM)
    bf16, f32 = jnp.bfloat16, jnp.float32
    dma = pltpu.SemaphoreType.DMA
    received, grad = pl.pallas_call(
        kernel,
        out_shape=(
            jax.ShapeDtypeStruct((EXPERTS, CAP, D), bf16),
            jax.ShapeDtypeStruct((16, BLOCK), f32),
        ),
        in_specs=[in_hbm] * 6,
        out_specs=(anywhere, pl.BlockSpec(memory_space=pltpu.VMEM)),
        scratch_shapes=[
            pltpu.VMEM((128, D), bf16),
            pltpu.VMEM((EXPERTS, 128), f32),
            pltpu.VMEM((2, 128), jnp.int32),
            pltpu.VMEM((2, 128), jnp.int32),
            pltpu.VMEM((16, D), bf16),
            pltpu.VMEM((16, EXPERTS * BLOCK), bf16),
            pltpu.VMEM((EXPERTS, CAP, D), bf16),
            pltpu.VMEM((ROW, 16, 2 * BLOCK + 128), bf16),
            pltpu.VMEM((ROW, 16, 2 * BLOCK + 128), bf16),
            pltpu.VMEM((ROLES, 4, 8, 128), f32),
            pltpu.VMEM((NZ, 4, 8, 128), f32),
            pltpu.VMEM((4, 8, 128), f32),
            pltpu.VMEM((NY, 4, 8, 128), f32),
            pltpu.VMEM((4, 8, 128), f32),
            pltpu.VMEM((2, 4, 8, 128), f32),
            dma((6,)), dma, pltpu.SemaphoreType.REGULAR, pltpu.SemaphoreType.REGULAR, pltpu.SemaphoreType.REGULAR,
            dma((EXPERTS, PARTS)), dma((EXPERTS, PARTS)),
            dma((ROW,)), dma((ROW,)),
            dma((ROLES,)), dma((NZ,)),
            dma((NY,)), dma((NY,)),
            dma((NZ,)), dma((2,)),
        ],
        compiler_params=pltpu.CompilerParams(
            collective_id=0, has_side_effects=True, vmem_limit_bytes=60 << 20
        ),
        cost_estimate=pl.CostEstimate(
            flops=300_000_000, bytes_accessed=8_000_000, transcendentals=256
        ),
    )(d_out, logits.T, routes.T, slots.T, state_map.T, channels)
    return received[None, None], grad


def solution(mesh):
    return jax.shard_map(
        shards,
        mesh=mesh,
        in_specs=(
            P(("dp", "expert"), None),
            P(("dp", "expert"), None),
            P(("dp", "expert"), None),
            P(("dp", "expert"), None),
            P(),
            P(("dp", "expert"), None),
        ),
        out_specs=(P("dp", "expert", None, None, None), P(None, "expert")),
        check_vma=False,
    )
```

```python
import jax
import jax.numpy as jnp
from jax import lax
from jax.experimental import pallas as pl
from jax.experimental.pallas import tpu as pltpu
from jax.sharding import PartitionSpec as P

MESH = pl.DeviceIdType.MESH
NX, NY, NZ, NC = 4, 8, 16, 2
EXPERTS, CAP, D = 16, 16, 4096
ROW = NX * NC
BLOCK = 512
TILE = 512

FAR = [(1, dx, dc) for dx in (2, 1, 3, 0) for dc in (0, 1)]
NEAR = [(0, dx, dc) for dx in (2, 1, 3, 0) for dc in (0, 1) if (dx, dc) != (0, 0)]
PEERS = FAR + NEAR
PARTS = 2
MIX = (FAR[:3] + NEAR[:1] + FAR[3:5] + NEAR[1:2] + FAR[5:7] + NEAR[2:3] + FAR[7:] + NEAR[3:])
BULK = [(*offsets, q) for q in range(PARTS) for offsets in MIX]
FIRST = 1
EXTRA = ((14, 14, 4),)
CUTS = (14, 26, 30)
DO_M = True
ALONG_Z = [s * k % NZ for k in range(1, 9) for s in (1, -1) if not (k == 8 and s < 0)]
ROLES = 4
ALONG_Y = (4, 3, 5, 2, 6, 1, 7)


def kernel(
    d_hbm, logits_hbm, routes_hbm, slots_hbm, map_hbm, channels_hbm,
    out, grad,
    d, logits, routes, slots, state_map, channels, pack,
    rows_out, rows_in, z_out, z_in, y_out, y_in, f_out, f_in,
    load_sem, own_sem, later, first, line, b_send, b_recv, r_send, r_recv, z_send, z_recv, y_send, y_recv, f_send, f_recv,
):
    dp, me = lax.axis_index("dp"), lax.axis_index("expert")
    z, y_lo = lax.rem(dp, NZ), dp // NZ
    y_hi, row = me // ROW, lax.rem(me, ROW)
    x, c = row // NC, lax.rem(row, NC)
    y = y_hi * 4 + y_lo

    def peer(dy, dx, dc, part=0):
        return (
            lax.rem(y_hi + dy, 2) * ROW + lax.rem(x + dx, NX) * NC + lax.rem(c + dc, NC)
        )

    def at_z(other):
        return (y_lo * NZ + other, me)

    def at_y(other):
        return (lax.rem(other, 4) * NZ + z, (other // 4) * ROW + row)

    barrier = pltpu.get_barrier_semaphore()

    def greet(device):
        pl.semaphore_signal(barrier, inc=1, device_id=device, device_id_type=MESH)

    corner = (row == 0) & (y == 0)
    rank = jnp.where(corner, lax.rem(z + NZ - 1, NZ), z)

    for offsets in PEERS:

        @pl.when(me != 0)
        def _():
            greet((dp, peer(*offsets)))

    for k in ALONG_Y:
        if k != 4:

            @pl.when(y != 0)
            def _():
                greet(at_y(lax.rem(y + k, NY)))

    for k in range(1, NZ):

        @pl.when(rank + k < NZ)
        def _():
            greet(at_z(lax.rem(z + k, NZ)))

    greeted = rank + jnp.where(me == 0, 15, 14) + jnp.where((y == 0) | (y == 4), 6, 5)

    loads = [
        pltpu.make_async_copy(source, target, load_sem.at[i])
        for i, (source, target) in enumerate(
            [
                (logits_hbm, logits),
                (routes_hbm, routes),
                (slots_hbm, slots),
                (d_hbm, d),
                (channels_hbm, channels),
                (map_hbm, state_map),
            ]
        )
    ]
    for load in loads:
        load.start()
    for load in loads[:3]:
        load.wait()

    expert_ids = lax.broadcasted_iota(jnp.int32, (EXPERTS, 128), 0)
    picked = [
        jnp.sum(
            jnp.where(expert_ids == routes[k : k + 1, :], logits[...], 0.0),
            axis=0,
            keepdims=True,
        )
        for k in range(2)
    ]
    weights = [
        jax.nn.sigmoid(picked[0] - picked[1]),
        jax.nn.sigmoid(picked[1] - picked[0]),
    ]
    target = [routes[k : k + 1, :] * CAP + slots[k : k + 1, :] for k in range(2)]

    def route(half):
        ids = lax.broadcasted_iota(jnp.int32, (128, 128), 0) + half * 128
        hit = [ids == target[k] for k in range(2)]
        chosen = jnp.where(hit[0] | hit[1], 1.0, 0.0).astype(jnp.bfloat16)
        scale = jnp.where(hit[0], weights[0], 0.0) + jnp.where(hit[1], weights[1], 0.0)
        return chosen, jnp.sum(scale, axis=1, keepdims=True)

    def pack_half(half):
        chosen, scale = route(half)
        for i in range(D // TILE):
            columns = slice(i * TILE, (i + 1) * TILE)
            rows = jnp.dot(chosen, d[:, columns], preferred_element_type=jnp.float32)
            pack[pl.ds(half * 8, 8), :, columns] = (
                (rows * scale).astype(jnp.bfloat16).reshape(8, CAP, TILE)
            )

    loads[3].wait()
    pack_half(1 - y_hi)

    loads[4].wait()
    loads[5].wait()
    state_cot = lax.dot_general(
        d[0:16, :], state_map[...], (((1,), (1,)), ((), ())),
        preferred_element_type=jnp.float32,
    ).astype(jnp.bfloat16)
    spread = (
        lax.broadcasted_iota(jnp.int32, (16, 128), 0)
        == lax.broadcasted_iota(jnp.int32, (16, 128), 1)
    ).astype(jnp.bfloat16)
    wide = jnp.dot(state_cot, spread, preferred_element_type=jnp.float32).astype(
        jnp.bfloat16
    )
    for i in range(ROW):
        for b in range(2):
            begin = (b * ROW + i) * BLOCK
            rows_out[i, :, b * BLOCK : (b + 1) * BLOCK] = channels[:, begin : begin + BLOCK]
        rows_out[i, :, 2 * BLOCK :] = wide

    pl.semaphore_wait(barrier, greeted)

    def tell(semaphore, device):
        pl.semaphore_signal(semaphore, inc=1, device_id=device, device_id_type=MESH)

    for offsets in PEERS:

        @pl.when(me == 0)
        def _():
            tell(first, (dp, peer(*offsets)))

    for k in ALONG_Y:
        if k != 4:

            @pl.when(y == 0)
            def _():
                tell(line, at_y(lax.rem(y + k, NY)))

    for k in range(1, NZ):

        @pl.when(k <= rank)
        def _():
            tell(later, at_z(lax.rem(z + NZ - k, NZ)))

    def send(source, destination, send_sem, recv_sem, device):
        copy = pltpu.make_async_remote_copy(
            src_ref=source,
            dst_ref=destination,
            send_sem=send_sem,
            recv_sem=recv_sem,
            device_id=device,
            device_id_type=MESH,
        )
        return copy

    def block(offsets, at):
        return to(peer(*offsets), offsets[3], at)

    def to(other, q, at):
        columns = pl.ds(q * (D // PARTS), D // PARTS)
        return send(
            pack.at[other, :, columns], out.at[at(other), :, columns],
            b_send.at[other, q], b_recv.at[at(other), q], (dp, other),
        )

    def to_first(q):
        return to(0, q, lambda other: me)

    def bulk(offsets):
        return block(offsets, lambda other: me)

    def bulk_in(offsets):
        return block(offsets, lambda other: other)

    def start(parts):
        for offsets in parts:

            @pl.when(peer(*offsets) != 0)
            def _():
                bulk(offsets).start()

    start(BULK[:FIRST])
    def across(other):
        return send(
            rows_out.at[other], rows_in.at[row], r_send.at[other], r_recv.at[row],
            (dp, y_hi * ROW + other),
        )

    for _, dx, dc in NEAR:
        other = lax.rem(x + dx, NX) * NC + lax.rem(c + dc, NC)

        @pl.when(y_hi * ROW + other != 0)
        def _():
            across(other).start()

    rows_in[row] = rows_out[row]
    pack_half(y_hi)
    own = pltpu.make_async_copy(pack.at[me], out.at[me], own_sem)
    own.start()
    start(BULK[FIRST : CUTS[0]])

    def extra(i, early):
        begin, end, below = EXTRA[i]

        @pl.when((z < below) == early)
        def _():
            start(BULK[begin:end])

    for i in range(len(EXTRA)):
        extra(i, True)

    @pl.when(me != 0)
    def _():
        pl.semaphore_wait(first, 1)

        @pl.when(y_hi == 0)
        def _():
            across(0).start()

        for q in range(PARTS):
            to_first(q).start()


    for _, dx, dc in NEAR:
        other = lax.rem(x + dx, NX) * NC + lax.rem(c + dc, NC)
        copy = send(
            rows_out.at[other], rows_in.at[other], r_send.at[other], r_recv.at[other],
            (dp, y_hi * ROW + other),
        )
        copy.wait_recv()
    cot = rows_in[:, :, 2 * BLOCK :].reshape(ROW * 16, 128)
    cot = cot.astype(jnp.float32).T[0:16, :].astype(jnp.bfloat16)
    partial = jnp.dot(
        cot, rows_in[:, :, : 2 * BLOCK].reshape(ROW * 16, 2 * BLOCK),
        preferred_element_type=jnp.float32,
    )
    for p in range(16):
        h, q = p // 8, p % 8
        z_out[p // 4, p % 4] = partial[h * 8 : (h + 1) * 8, q * 128 : (q + 1) * 128]

    adds = z < ROLES
    wait_now = adds | corner

    @pl.when(wait_now & (rank < NZ - 1))
    def _():
        pl.semaphore_wait(later, NZ - 1 - rank)

    def along(to):
        return send(z_out.at[to], z_in.at[z], z_send.at[to], z_recv.at[z], at_z(to))

    for to_z in range(ROLES):

        @pl.when(z != to_z)
        def _():
            along(to_z).start()

    for i in range(len(EXTRA)):
        extra(i, False)
    start(BULK[EXTRA[-1][1] : CUTS[1]])
    @pl.when((y != 0) & (y != 4))
    def _():
        pl.semaphore_wait(line, 1)

    half = lax.rem(z, 2)

    def upright(other):
        return send(y_out, y_in.at[y], y_send.at[other], y_recv.at[y], at_y(other))

    @pl.when(adds)
    def _():
        z_in[z] = z_out[lax.rem(z, ROLES)]
        for k in ALONG_Z:
            other = lax.rem(z + k, NZ)
            send(z_out.at[0], z_in.at[other], z_send.at[0], z_recv.at[other], at_z(other)).wait_recv()
        total = jnp.sum(z_in[...], axis=0)
        y_out[...] = total
        for k in ALONG_Y:
            other = lax.rem(y + k, NY)

            @pl.when(other // 4 == half)
            def _():
                upright(other).start()

        y_in[y] = total

    start(BULK[CUTS[1] : CUTS[2]])

    gives = adds & (y_hi == half)

    def back(other):
        return send(f_out, f_in.at[z // 2], f_send.at[other], f_recv.at[z // 2], at_z(other))

    @pl.when(gives)
    def _():
        for k in ALONG_Y:
            other = lax.rem(y + k, NY)
            send(y_out, y_in.at[other], y_send.at[other], y_recv.at[other], at_y(other)).wait_recv()
        summed = jnp.sum(y_in[...], axis=0)
        f_out[...] = summed
        for to_z in range(NZ):

            @pl.when(z != to_z)
            def _():
                back(to_z).start()

        f_in[z // 2] = summed

    start(BULK[CUTS[2] :])

    for h in range(2):
        giver = 2 * h + y_hi

        @pl.when(giver != z)
        def _():
            send(f_out, f_in.at[h], f_send.at[0], f_recv.at[h], at_z(giver)).wait_recv()

    for p in range(8):
        h, q = p // 4, p % 4
        grad[h * 8 : (h + 1) * 8, q * 128 : (q + 1) * 128] = f_in[h, q]

    @pl.when(jnp.logical_not(wait_now) & (rank < NZ - 1))
    def _():
        pl.semaphore_wait(later, NZ - 1 - rank)

    for _, dx, dc in NEAR:
        across(lax.rem(x + dx, NX) * NC + lax.rem(c + dc, NC)).wait_send()
    for to_z in range(ROLES):

        @pl.when(z != to_z)
        def _():
            along(to_z).wait_send()

    for k in ALONG_Y:
        other = lax.rem(y + k, NY)

        @pl.when(adds & (other // 4 == half))
        def _():
            upright(other).wait_send()

    @pl.when(gives)
    def _():
        for k in ALONG_Z:
            back(lax.rem(z + k, NZ)).wait_send()

    own.wait()
    for offsets in BULK:
        bulk(offsets).wait_send()
        bulk_in(offsets).wait_recv()


def shards(d_out, logits, routes, slots, state_map, channels):
    anywhere = pl.BlockSpec(memory_space=pl.ANY)
    in_hbm = pl.BlockSpec(memory_space=pltpu.HBM)
    bf16, f32 = jnp.bfloat16, jnp.float32
    dma = pltpu.SemaphoreType.DMA
    received, grad = pl.pallas_call(
        kernel,
        out_shape=(
            pltpu.VMEM((EXPERTS, CAP, D), bf16),
            pltpu.VMEM((16, BLOCK), f32),
        ),
        in_specs=[in_hbm] * 6,
        out_specs=(anywhere, pl.BlockSpec(memory_space=pltpu.VMEM)),
        scratch_shapes=[
            pltpu.VMEM((128, D), bf16),
            pltpu.VMEM((EXPERTS, 128), f32),
            pltpu.VMEM((2, 128), jnp.int32),
            pltpu.VMEM((2, 128), jnp.int32),
            pltpu.VMEM((16, D), bf16),
            pltpu.VMEM((16, EXPERTS * BLOCK), bf16),
            pltpu.VMEM((EXPERTS, CAP, D), bf16),
            pltpu.VMEM((ROW, 16, 2 * BLOCK + 128), bf16),
            pltpu.VMEM((ROW, 16, 2 * BLOCK + 128), bf16),
            pltpu.VMEM((ROLES, 4, 8, 128), f32),
            pltpu.VMEM((NZ, 4, 8, 128), f32),
            pltpu.VMEM((4, 8, 128), f32),
            pltpu.VMEM((NY, 4, 8, 128), f32),
            pltpu.VMEM((4, 8, 128), f32),
            pltpu.VMEM((2, 4, 8, 128), f32),
            dma((6,)), dma, pltpu.SemaphoreType.REGULAR, pltpu.SemaphoreType.REGULAR, pltpu.SemaphoreType.REGULAR,
            dma((EXPERTS, PARTS)), dma((EXPERTS, PARTS)),
            dma((ROW,)), dma((ROW,)),
            dma((ROLES,)), dma((NZ,)),
            dma((NY,)), dma((NY,)),
            dma((NZ,)), dma((2,)),
        ],
        compiler_params=pltpu.CompilerParams(
            collective_id=0, has_side_effects=True, vmem_limit_bytes=60 << 20
        ),
        cost_estimate=pl.CostEstimate(
            flops=300_000_000, bytes_accessed=8_000_000, transcendentals=256
        ),
    )(d_out, logits.T, routes.T, slots.T, state_map.T, channels)
    return received[None, None], grad


def solution(mesh):
    return jax.shard_map(
        shards,
        mesh=mesh,
        in_specs=(
            P(("dp", "expert"), None),
            P(("dp", "expert"), None),
            P(("dp", "expert"), None),
            P(("dp", "expert"), None),
            P(),
            P(("dp", "expert"), None),
        ),
        out_specs=(P("dp", "expert", None, None, None), P(None, "expert")),
        check_vma=False,
    )
```

```python
import jax
import jax.numpy as jnp
from jax import lax
from jax.experimental import pallas as pl
from jax.experimental.pallas import tpu as pltpu
from jax.sharding import PartitionSpec as P

MESH = pl.DeviceIdType.MESH
NX, NY, NZ, NC = 4, 8, 16, 2
EXPERTS, CAP, D = 16, 16, 4096
ROW = NX * NC
BLOCK = 512
TILE = 512

FAR = [(1, dx, dc) for dx in (2, 1, 3, 0) for dc in (0, 1)]
NEAR = [(0, dx, dc) for dx in (2, 1, 3, 0) for dc in (0, 1) if (dx, dc) != (0, 0)]
PEERS = FAR + NEAR
PARTS = 2
MIX = (FAR[:3] + NEAR[:1] + FAR[3:5] + NEAR[1:2] + FAR[5:7] + NEAR[2:3] + FAR[7:] + NEAR[3:])
BULK = [(*offsets, q) for q in range(PARTS) for offsets in MIX]
FIRST = 1
EXTRA = ((18, 18, 2),)
CUTS = (18, 30, 30)
DO_M = True
ALONG_Z = [s * k % NZ for k in range(1, 9) for s in (1, -1) if not (k == 8 and s < 0)]
ROLES = 2
ALONG_Y = (4, 3, 5, 2, 6, 1, 7)


def kernel(
    d_hbm, logits_hbm, routes_hbm, slots_hbm, map_hbm, channels_hbm,
    out, grad,
    d, logits, routes, slots, state_map, channels, pack,
    rows_out, rows_in, z_out, z_in, y_out, y_in, f_out, f_in,
    load_sem, own_sem, later, first, line, b_send, b_recv, r_send, r_recv, z_send, z_recv, y_send, y_recv, f_send, f_recv,
):
    dp, me = lax.axis_index("dp"), lax.axis_index("expert")
    z, y_lo = lax.rem(dp, NZ), dp // NZ
    y_hi, row = me // ROW, lax.rem(me, ROW)
    x, c = row // NC, lax.rem(row, NC)
    y = y_hi * 4 + y_lo

    def peer(dy, dx, dc, part=0):
        return (
            lax.rem(y_hi + dy, 2) * ROW + lax.rem(x + dx, NX) * NC + lax.rem(c + dc, NC)
        )

    def at_z(other):
        return (y_lo * NZ + other, me)

    def at_y(other):
        return (lax.rem(other, 4) * NZ + z, (other // 4) * ROW + row)

    barrier = pltpu.get_barrier_semaphore()

    def greet(device):
        pl.semaphore_signal(barrier, inc=1, device_id=device, device_id_type=MESH)

    corner = (row == 0) & (y == 0)
    rank = jnp.where(corner, lax.rem(z + NZ - 1, NZ), z)

    for offsets in PEERS:

        @pl.when(me != 0)
        def _():
            greet((dp, peer(*offsets)))

    for k in ALONG_Y:
        if k != 4:

            @pl.when(y != 0)
            def _():
                greet(at_y(lax.rem(y + k, NY)))

    for k in range(1, NZ):

        @pl.when(rank + k < NZ)
        def _():
            greet(at_z(lax.rem(z + k, NZ)))

    greeted = rank + jnp.where(me == 0, 15, 14) + jnp.where((y == 0) | (y == 4), 6, 5)

    loads = [
        pltpu.make_async_copy(source, target, load_sem.at[i])
        for i, (source, target) in enumerate(
            [
                (logits_hbm, logits),
                (routes_hbm, routes),
                (slots_hbm, slots),
                (d_hbm, d),
                (channels_hbm, channels),
                (map_hbm, state_map),
            ]
        )
    ]
    for load in loads:
        load.start()
    for load in loads[:3]:
        load.wait()

    expert_ids = lax.broadcasted_iota(jnp.int32, (EXPERTS, 128), 0)
    picked = [
        jnp.sum(
            jnp.where(expert_ids == routes[k : k + 1, :], logits[...], 0.0),
            axis=0,
            keepdims=True,
        )
        for k in range(2)
    ]
    weights = [
        jax.nn.sigmoid(picked[0] - picked[1]),
        jax.nn.sigmoid(picked[1] - picked[0]),
    ]
    target = [routes[k : k + 1, :] * CAP + slots[k : k + 1, :] for k in range(2)]

    def route(half):
        ids = lax.broadcasted_iota(jnp.int32, (128, 128), 0) + half * 128
        hit = [ids == target[k] for k in range(2)]
        chosen = jnp.where(hit[0] | hit[1], 1.0, 0.0).astype(jnp.bfloat16)
        scale = jnp.where(hit[0], weights[0], 0.0) + jnp.where(hit[1], weights[1], 0.0)
        return chosen, jnp.sum(scale, axis=1, keepdims=True)

    def pack_half(half):
        chosen, scale = route(half)
        for i in range(D // TILE):
            columns = slice(i * TILE, (i + 1) * TILE)
            rows = jnp.dot(chosen, d[:, columns], preferred_element_type=jnp.float32)
            pack[pl.ds(half * 8, 8), :, columns] = (
                (rows * scale).astype(jnp.bfloat16).reshape(8, CAP, TILE)
            )

    loads[3].wait()
    pack_half(1 - y_hi)

    loads[4].wait()
    loads[5].wait()
    state_cot = lax.dot_general(
        d[0:16, :], state_map[...], (((1,), (1,)), ((), ())),
        preferred_element_type=jnp.float32,
    ).astype(jnp.bfloat16)
    spread = (
        lax.broadcasted_iota(jnp.int32, (16, 128), 0)
        == lax.broadcasted_iota(jnp.int32, (16, 128), 1)
    ).astype(jnp.bfloat16)
    wide = jnp.dot(state_cot, spread, preferred_element_type=jnp.float32).astype(
        jnp.bfloat16
    )
    for i in range(ROW):
        for b in range(2):
            begin = (b * ROW + i) * BLOCK
            rows_out[i, :, b * BLOCK : (b + 1) * BLOCK] = channels[:, begin : begin + BLOCK]
        rows_out[i, :, 2 * BLOCK :] = wide

    pl.semaphore_wait(barrier, greeted)

    def tell(semaphore, device):
        pl.semaphore_signal(semaphore, inc=1, device_id=device, device_id_type=MESH)

    for offsets in PEERS:

        @pl.when(me == 0)
        def _():
            tell(first, (dp, peer(*offsets)))

    for k in ALONG_Y:
        if k != 4:

            @pl.when(y == 0)
            def _():
                tell(line, at_y(lax.rem(y + k, NY)))

    for k in range(1, NZ):

        @pl.when(k <= rank)
        def _():
            tell(later, at_z(lax.rem(z + NZ - k, NZ)))

    def send(source, destination, send_sem, recv_sem, device):
        copy = pltpu.make_async_remote_copy(
            src_ref=source,
            dst_ref=destination,
            send_sem=send_sem,
            recv_sem=recv_sem,
            device_id=device,
            device_id_type=MESH,
        )
        return copy

    def block(offsets, at):
        return to(peer(*offsets), offsets[3], at)

    def to(other, q, at):
        columns = pl.ds(q * (D // PARTS), D // PARTS)
        return send(
            pack.at[other, :, columns], out.at[at(other), :, columns],
            b_send.at[other, q], b_recv.at[at(other), q], (dp, other),
        )

    def to_first(q):
        return to(0, q, lambda other: me)

    def bulk(offsets):
        return block(offsets, lambda other: me)

    def bulk_in(offsets):
        return block(offsets, lambda other: other)

    def start(parts):
        for offsets in parts:

            @pl.when(peer(*offsets) != 0)
            def _():
                bulk(offsets).start()

    start(BULK[:FIRST])
    def across(other):
        return send(
            rows_out.at[other], rows_in.at[row], r_send.at[other], r_recv.at[row],
            (dp, y_hi * ROW + other),
        )

    for _, dx, dc in NEAR:
        other = lax.rem(x + dx, NX) * NC + lax.rem(c + dc, NC)

        @pl.when(y_hi * ROW + other != 0)
        def _():
            across(other).start()

    rows_in[row] = rows_out[row]
    pack_half(y_hi)
    own = pltpu.make_async_copy(pack.at[me], out.at[me], own_sem)
    own.start()
    start(BULK[FIRST : CUTS[0]])

    def extra(i, early):
        begin, end, below = EXTRA[i]

        @pl.when((z < below) == early)
        def _():
            start(BULK[begin:end])

    for i in range(len(EXTRA)):
        extra(i, True)

    @pl.when(me != 0)
    def _():
        pl.semaphore_wait(first, 1)

        @pl.when(y_hi == 0)
        def _():
            across(0).start()

        for q in range(PARTS):
            to_first(q).start()


    for _, dx, dc in NEAR:
        other = lax.rem(x + dx, NX) * NC + lax.rem(c + dc, NC)
        copy = send(
            rows_out.at[other], rows_in.at[other], r_send.at[other], r_recv.at[other],
            (dp, y_hi * ROW + other),
        )
        copy.wait_recv()
    cot = rows_in[:, :, 2 * BLOCK :].reshape(ROW * 16, 128)
    cot = cot.astype(jnp.float32).T[0:16, :].astype(jnp.bfloat16)
    partial = jnp.dot(
        cot, rows_in[:, :, : 2 * BLOCK].reshape(ROW * 16, 2 * BLOCK),
        preferred_element_type=jnp.float32,
    )
    for p in range(16):
        h, q = p // 8, p % 8
        z_out[h, q // 4, q % 4] = partial[h * 8 : (h + 1) * 8, q * 128 : (q + 1) * 128]

    adds = z < ROLES
    wait_now = adds | corner

    @pl.when(wait_now & (rank < NZ - 1))
    def _():
        pl.semaphore_wait(later, NZ - 1 - rank)

    def along(to):
        return send(z_out.at[to], z_in.at[z], z_send.at[to], z_recv.at[z], at_z(to))

    for to_z in range(ROLES):

        @pl.when(z != to_z)
        def _():
            along(to_z).start()

    for i in range(len(EXTRA)):
        extra(i, False)
    start(BULK[EXTRA[-1][1] : CUTS[1]])
    @pl.when((y != 0) & (y != 4))
    def _():
        pl.semaphore_wait(line, 1)

    def upright(other):
        return send(y_out.at[other // 4], y_in.at[y], y_send.at[other], y_recv.at[y], at_y(other))

    @pl.when(adds)
    def _():
        z_in[z] = z_out[lax.rem(z, ROLES)]
        for k in ALONG_Z:
            other = lax.rem(z + k, NZ)
            send(z_out.at[0], z_in.at[other], z_send.at[0], z_recv.at[other], at_z(other)).wait_recv()
        total = jnp.sum(z_in[...], axis=0)
        y_out[...] = total
        for k in ALONG_Y:
            upright(lax.rem(y + k, NY)).start()
        y_in[y] = jnp.where(y_hi == 0, total[0], total[1])

    start(BULK[CUTS[1] : CUTS[2]])

    mine = lax.rem(z, ROLES)

    def back(other):
        return send(f_out, f_in.at[mine], f_send.at[other], f_recv.at[mine], at_z(other))

    @pl.when(adds)
    def _():
        for k in ALONG_Y:
            other = lax.rem(y + k, NY)
            send(y_out.at[0], y_in.at[other], y_send.at[other], y_recv.at[other], at_y(other)).wait_recv()
        summed = jnp.sum(y_in[...], axis=0)
        f_out[...] = summed
        for to_z in range(NZ):

            @pl.when(z != to_z)
            def _():
                back(to_z).start()

        f_in[mine] = summed

    start(BULK[CUTS[2] :])

    for h in range(2):

        @pl.when(z != h)
        def _():
            send(f_out, f_in.at[h], f_send.at[0], f_recv.at[h], at_z(h)).wait_recv()

    for p in range(8):
        h, q = p // 4, p % 4
        grad[h * 8 : (h + 1) * 8, q * 128 : (q + 1) * 128] = f_in[h, q]

    @pl.when(jnp.logical_not(wait_now) & (rank < NZ - 1))
    def _():
        pl.semaphore_wait(later, NZ - 1 - rank)

    for _, dx, dc in NEAR:
        across(lax.rem(x + dx, NX) * NC + lax.rem(c + dc, NC)).wait_send()
    for to_z in range(ROLES):

        @pl.when(z != to_z)
        def _():
            along(to_z).wait_send()

    @pl.when(adds)
    def _():
        for k in ALONG_Y:
            upright(lax.rem(y + k, NY)).wait_send()
        for k in ALONG_Z:
            back(lax.rem(z + k, NZ)).wait_send()

    own.wait()
    for offsets in BULK:
        bulk(offsets).wait_send()
        bulk_in(offsets).wait_recv()


def shards(d_out, logits, routes, slots, state_map, channels):
    anywhere = pl.BlockSpec(memory_space=pl.ANY)
    in_hbm = pl.BlockSpec(memory_space=pltpu.HBM)
    bf16, f32 = jnp.bfloat16, jnp.float32
    dma = pltpu.SemaphoreType.DMA
    received, grad = pl.pallas_call(
        kernel,
        out_shape=(
            pltpu.VMEM((EXPERTS, CAP, D), bf16),
            pltpu.VMEM((16, BLOCK), f32),
        ),
        in_specs=[in_hbm] * 6,
        out_specs=(anywhere, pl.BlockSpec(memory_space=pltpu.VMEM)),
        scratch_shapes=[
            pltpu.VMEM((128, D), bf16),
            pltpu.VMEM((EXPERTS, 128), f32),
            pltpu.VMEM((2, 128), jnp.int32),
            pltpu.VMEM((2, 128), jnp.int32),
            pltpu.VMEM((16, D), bf16),
            pltpu.VMEM((16, EXPERTS * BLOCK), bf16),
            pltpu.VMEM((EXPERTS, CAP, D), bf16),
            pltpu.VMEM((ROW, 16, 2 * BLOCK + 128), bf16),
            pltpu.VMEM((ROW, 16, 2 * BLOCK + 128), bf16),
            pltpu.VMEM((ROLES, 2, 4, 8, 128), f32),
            pltpu.VMEM((NZ, 2, 4, 8, 128), f32),
            pltpu.VMEM((2, 4, 8, 128), f32),
            pltpu.VMEM((NY, 4, 8, 128), f32),
            pltpu.VMEM((4, 8, 128), f32),
            pltpu.VMEM((2, 4, 8, 128), f32),
            dma((6,)), dma, pltpu.SemaphoreType.REGULAR, pltpu.SemaphoreType.REGULAR, pltpu.SemaphoreType.REGULAR,
            dma((EXPERTS, PARTS)), dma((EXPERTS, PARTS)),
            dma((ROW,)), dma((ROW,)),
            dma((ROLES,)), dma((NZ,)),
            dma((NY,)), dma((NY,)),
            dma((NZ,)), dma((2,)),
        ],
        compiler_params=pltpu.CompilerParams(
            collective_id=0, has_side_effects=True, vmem_limit_bytes=60 << 20
        ),
        cost_estimate=pl.CostEstimate(
            flops=300_000_000, bytes_accessed=8_000_000, transcendentals=256
        ),
    )(d_out, logits.T, routes.T, slots.T, state_map.T, channels)
    return received[None, None], grad


def solution(mesh):
    return jax.shard_map(
        shards,
        mesh=mesh,
        in_specs=(
            P(("dp", "expert"), None),
            P(("dp", "expert"), None),
            P(("dp", "expert"), None),
            P(("dp", "expert"), None),
            P(),
            P(("dp", "expert"), None),
        ),
        out_specs=(P("dp", "expert", None, None, None), P(None, "expert")),
        check_vma=False,
    )
```
